32 devices in a mesh: groups: 2 (over x), row: 8 (over z, y), col: 2 (over core).
Axes of the slice: x: 2, y: 2, z: 4, core: 2. Of those that a mesh axis runs over, the one named last changes fastest.
Arguments:
- activations: bfloat16 [4096, 8192], P(('groups', 'row'), 'col'), parts along dimension 0, may hold values from -6 to 6
- output_gradient: bfloat16 [4096, 16384], P(('groups', 'col'), 'row'), parts along dimension 0, may hold values from -6 to 6
- frozen_weight: bfloat16 [8192, 16384], P('col', 'row'), may hold values from -0.046875 to 0.046875
- adapter_down_maps: bfloat16 [64, 16, 8192], P(None, None, ('col', 'row')), may hold values from -0.25 to 0.25
- adapter_up_maps: bfloat16 [64, 16, 16384], P(None, None, 'row'), may hold values from -0.046875 to 0.046875
- adapter_of_block: int32 [32], P('groups'), parts along dimension 0, may hold values from 0 to 63
- adapter_grad_slot: int32 [64], replicated, may hold values from 0 to 63, each once
Outputs:
- input_grad: bfloat16 [4096, 8192], P(('groups', 'row'), 'col'), parts along dimension 0
- down_grad: bfloat16 [128, 16, 8192], P(('groups', 'row'), None, 'col'), parts along dimension 0
- up_grad: bfloat16 [128, 16, 16384], P(('groups', 'col'), None, 'row'), parts along dimension 0
The draws below stay inside these ranges and needn't reach their ends.
There are 2 independent parts, one for each index of `groups`. The reference program is written for one: setup_inputs(seed, part) draws one part's arguments, and reference() takes and returns one part's arrays. A program takes and returns all parts, laid end to end along the dimension named above; an argument that names none is the same for every part. Nothing has to cross between parts.
Inputs may be any that keep to these rules, and one draw needn't show every extreme that they name: adapter_grad_slot holds every number below 64 once; slot s belongs to the adapter a with adapter_grad_slot[a] = s.
All inputs are finite; a program needn't handle non-finite values.
Results may differ from the reference program's by a relative error of at most 0.015.
Values may be sent and summed in bfloat16 or wider, within the bound.
A program may use at most 192 MiB of HBM per device.

```python
import math
import jax
import jax.numpy as jnp
import numpy as np
from jax import lax

INPUT_FEATURES = 8192
MODEL_WIDTH = 16384
ADAPTER_RANK = 16
ADAPTER_COUNT = 64
BLOCK = 128
NBLK = 16
TOKEN_COUNT = 2048
N_ROW = 8
N_COL = 2


def touch_ends(entries, rng, low, largest):
    index_at = [jax.random.randint(jax.random.fold_in(rng, axis), (), 0, length) for axis, length in enumerate(entries.shape)]
    widest = entries.shape.index(max(entries.shape))
    neighbour = index_at[:widest] + [(index_at[widest] + 1) % entries.shape[widest]] + index_at[widest + 1:]
    return entries.at[tuple(index_at)].set(low).at[tuple(neighbour)].set(largest)


def with_spikes(entries, own_key, source, target, parts, factor):
    owner, partner = [(jnp.arange(entries.shape[position]) // (entries.shape[position] // parts)).reshape([-1 if axis == position else 1 for axis in range(entries.ndim)]) for position in (source, target)]
    chosen = jax.random.permutation(own_key, parts)[partner]
    strong = (owner == chosen) | (owner == (partner + parts // 2) % parts)
    return jnp.where(strong, factor * entries, entries)


def steps_of(rng, extent, split, smallest, high):
    loudness, own = 1.0, jax.random.fold_in(rng, 6)
    for dim, parts in split:
        steps = jnp.exp(jax.random.uniform(jax.random.fold_in(own, dim), (parts,), jnp.float32, smallest / len(split), high / len(split)))
        loudness = loudness * jnp.repeat(steps, extent[dim] // parts).reshape([-1 if axis == dim else 1 for axis in range(len(extent))])
    return loudness


def cumulative_ranks(count, skew):
    weights = [(1 << 20) // math.isqrt(grade ** skew) + 1 for grade in range(1, count + 1)]
    deviation = 1 + sum(weights) // (1 << 30)
    return np.cumsum(np.array([max(1, weight // deviation) for weight in weights]))


def ranked_ids(key, shape, count, slope):
    table = cumulative_ranks(count, slope)
    ticket = jax.random.randint(jax.random.fold_in(key, 1), shape, 0, int(table[count - 1]))
    rank = jnp.searchsorted(jnp.asarray(table, jnp.int32), ticket, side="right")
    return jax.random.permutation(jax.random.fold_in(key, 2), count)[rank].astype(jnp.int32)


def noise(own_key, extent, width, limit, split=(), kind=jnp.bfloat16):
    entries = jax.random.normal(own_key, extent, jnp.float32) * width
    if len(split) > 0:
        entries = steps_of(own_key, extent, split, -0.22, 0.18) * entries
    return jnp.clip(entries, min=-limit, max=limit).astype(kind)


def bell_draw_with(key, dims, spread, most, pieces, heavy, kind=jnp.bfloat16):
    drawn = spread * jax.random.normal(key, dims, jnp.float32)
    if pieces:
        drawn = drawn * steps_of(key, dims, pieces, -0.22, 0.18)
    return jnp.clip(with_spikes(drawn, jax.random.fold_in(key, 3), *heavy), -most, most).astype(kind)


def setup_inputs(seed: int = 0, part: int = 0) -> dict:
    key_of = jax.random.split(jax.random.key(seed), 8)
    part_splits = jax.random.split(jax.random.fold_in(key_of[7], part), 8)
    activations = noise(part_splits[0], (TOKEN_COUNT, INPUT_FEATURES), 1.0, 6.0, ((0, 8), (1, 2)))
    output_gradient = bell_draw_with(part_splits[1], (TOKEN_COUNT, MODEL_WIDTH), 1.0, 6.0, ((0, 2), (1, 8)), (1, 0, 8, 2.0))
    frozen_weight = noise(key_of[2], (INPUT_FEATURES, MODEL_WIDTH), MODEL_WIDTH ** -0.5, 0.046875, ((0, 2), (1, 8)))
    adapter_down_maps = noise(key_of[3], (ADAPTER_COUNT, ADAPTER_RANK, INPUT_FEATURES), (INPUT_FEATURES // 16) ** -0.5, 0.25, ((2, 16),))
    adapter_up_maps = noise(key_of[4], (ADAPTER_COUNT, ADAPTER_RANK, MODEL_WIDTH), MODEL_WIDTH ** -0.5, 0.046875, ((2, 8),))
    adapter_of_block = touch_ends(ranked_ids(part_splits[5], (NBLK,), ADAPTER_COUNT, 2), jax.random.fold_in(part_splits[5], 3), 0, ADAPTER_COUNT - 1).astype(jnp.int32)
    adapter_grad_slot = jax.random.permutation(key_of[6], ADAPTER_COUNT).astype(jnp.int32)
    return {"activations": activations, "output_gradient": output_gradient, "frozen_weight": frozen_weight, "adapter_down_maps": adapter_down_maps, "adapter_up_maps": adapter_up_maps, "adapter_of_block": adapter_of_block, "adapter_grad_slot": adapter_grad_slot}


SCALE = 2.0
HIGH_PRECISION = lax.Precision.HIGHEST


def reference(activations, output_gradient, frozen_weight, adapter_down_maps, adapter_up_maps, adapter_of_block, adapter_grad_slot):
    blocks = TOKEN_COUNT // BLOCK
    x_blocks = activations.reshape(blocks, BLOCK, INPUT_FEATURES).astype(jnp.float32)
    dy_blocks = output_gradient.reshape(blocks, BLOCK, MODEL_WIDTH).astype(jnp.float32)
    selected_down = adapter_down_maps[adapter_of_block].astype(jnp.float32)
    selected_up = adapter_up_maps[adapter_of_block].astype(jnp.float32)
    hidden = jnp.einsum('btd,brd->btr', x_blocks, selected_down, precision=HIGH_PRECISION)
    back = SCALE * jnp.einsum('bto,bro->btr', dy_blocks, selected_up, precision=HIGH_PRECISION)
    hidden_low = hidden.astype(jnp.bfloat16).astype(jnp.float32)
    backward_low_rank = back.astype(jnp.bfloat16).astype(jnp.float32)
    adapter_term = jnp.einsum('efs,esl->efl', backward_low_rank, selected_down, precision=HIGH_PRECISION).reshape(TOKEN_COUNT, INPUT_FEATURES)
    token_slab = INPUT_FEATURES // (N_COL * N_ROW)
    width_out = MODEL_WIDTH // N_ROW
    owning_row = ((jnp.arange(INPUT_FEATURES, dtype=jnp.int32) % (INPUT_FEATURES // N_COL)) // token_slab).astype(jnp.int32)

    def one_shard(total, index_of_shard):
        dy_part = lax.dynamic_slice_in_dim(output_gradient, index_of_shard * width_out, width_out, 1)
        w_part = lax.dynamic_slice_in_dim(frozen_weight, index_of_shard * width_out, width_out, 1)
        partial_term = lax.dot_general(dy_part, w_part, (((1,), (1,)), ((), ())), preferred_element_type=jnp.float32)
        partial_term = partial_term + jnp.where((owning_row == index_of_shard)[None, :], adapter_term, jnp.float32(0.0))
        rounded = lax.optimization_barrier(partial_term.astype(jnp.bfloat16))
        return total + rounded.astype(jnp.float32), None

    total, _ = lax.scan(one_shard, jnp.zeros((TOKEN_COUNT, INPUT_FEATURES), jnp.float32), jnp.arange(N_ROW, dtype=jnp.int32))
    input_grad = total.astype(jnp.bfloat16)
    slot_of_block = adapter_grad_slot[adapter_of_block]
    choose = (slot_of_block[None, :] == jnp.arange(ADAPTER_COUNT, dtype=jnp.int32)[:, None]).astype(jnp.float32)
    down_parts = jnp.einsum('btr,btd->brd', backward_low_rank, x_blocks, precision=HIGH_PRECISION)
    down_grad = (jnp.einsum('sb,brd->srd', choose, down_parts, precision=HIGH_PRECISION) / BLOCK).astype(jnp.bfloat16)
    up_parts = jnp.einsum('btr,bto->bro', hidden_low, dy_blocks, precision=HIGH_PRECISION)
    up_grad = (SCALE / BLOCK * jnp.einsum('sb,bro->sro', choose, up_parts, precision=HIGH_PRECISION)).astype(jnp.bfloat16)
    return input_grad, down_grad, up_grad
```

```python
import jax
import jax.numpy as jnp
from jax import lax
from jax.sharding import PartitionSpec as P

BLOCK = 128


SCALE = 2.0
HIGH_PRECISION = lax.Precision.HIGHEST


def general_shards(
    activations,
    output_gradient,
    frozen_weight,
    adapter_down_maps,
    adapter_up_maps,
    adapter_of_block,
    adapter_grad_slot,
):
    n_row = lax.axis_size("row")
    n_col = lax.axis_size("col")
    index_of_row = lax.axis_index("row")
    col_index = lax.axis_index("col")
    adapter_list = adapter_down_maps.shape[0]
    rank_width = adapter_down_maps.shape[1]
    token_slab = adapter_down_maps.shape[2]
    width_out = output_gradient.shape[1]
    half_blocks = output_gradient.shape[0] // BLOCK
    blocks = half_blocks * n_col
    every_token = blocks * BLOCK
    dy_panel = lax.all_gather(output_gradient, "col", axis=0, tiled=True)
    x_columns = lax.all_to_all(activations, "row", split_axis=1, concat_axis=0, tiled=True)
    x_blocks = x_columns.reshape(blocks, BLOCK, token_slab)
    selected_down = adapter_down_maps[adapter_of_block]
    selected_up = adapter_up_maps[adapter_of_block]
    hidden_part = jnp.einsum(
        "btd,brd->btr", x_blocks, selected_down, preferred_element_type=jnp.float32
    )
    own_dy = output_gradient.reshape(half_blocks, BLOCK, width_out)
    own_up = lax.dynamic_slice_in_dim(selected_up, col_index * half_blocks, half_blocks, 0)
    back_own = jnp.einsum("bto,bro->btr", own_dy, own_up, preferred_element_type=jnp.float32)
    back_zero = jnp.zeros((blocks, BLOCK, rank_width), jnp.float32)
    back_part = lax.dynamic_update_slice_in_dim(back_zero, back_own, col_index * half_blocks, 0)
    hidden, back_sum = lax.psum((hidden_part, back_part), ("row", "col"))
    back = SCALE * back_sum
    hidden_low = hidden.astype(jnp.bfloat16)
    backward_low_rank = back.astype(jnp.bfloat16)
    adapter_token_slab = jnp.einsum(
        "efs,esl->efl", backward_low_rank, selected_down, preferred_element_type=jnp.float32
    )
    adapter_token_slab = adapter_token_slab.reshape(every_token, token_slab)
    partial_term = lax.dot_general(
        dy_panel, frozen_weight, (((1,), (1,)), ((), ())), preferred_element_type=jnp.float32
    )
    present_value = lax.dynamic_slice_in_dim(partial_term, index_of_row * token_slab, token_slab, 1)
    input_grad = lax.psum_scatter(
        lax.dynamic_update_slice_in_dim(
            partial_term, present_value + adapter_token_slab, index_of_row * token_slab, 1
        ).astype(jnp.bfloat16),
        "row",
        scatter_dimension=0,
        tiled=True,
    )
    slot_of_block = adapter_grad_slot[adapter_of_block]
    down_parts = jnp.einsum(
        "btr,btd->brd", backward_low_rank, x_blocks, preferred_element_type=jnp.float32
    )
    per_row = adapter_list // n_row
    own_slots = index_of_row * per_row + jnp.arange(per_row, dtype=jnp.int32)
    choose_own = (slot_of_block[None, :] == own_slots[:, None]).astype(jnp.float32)
    summed = jnp.einsum(
        "sb,brd->srd",
        choose_own,
        lax.all_gather(down_parts.astype(jnp.bfloat16), "row", axis=2, tiled=True).astype(
            jnp.float32
        ),
        precision=HIGH_PRECISION,
    )
    down_grad = (summed / BLOCK).astype(jnp.bfloat16)
    own_hidden = lax.dynamic_slice_in_dim(hidden_low, col_index * half_blocks, half_blocks, 0)
    own_cotangent = output_gradient.reshape(half_blocks, BLOCK, width_out)
    up_parts = jnp.einsum(
        "btr,bto->bro", own_hidden, own_cotangent, preferred_element_type=jnp.float32
    )
    every_block = lax.all_gather(up_parts.astype(jnp.bfloat16), "col", axis=0, tiled=True).astype(
        up_parts.dtype
    )
    per_col = adapter_list // n_col
    col_slots = col_index * per_col + jnp.arange(per_col, dtype=jnp.int32)
    choose_col = (slot_of_block[None, :] == col_slots[:, None]).astype(jnp.float32)
    up_grad = (
        SCALE / BLOCK * jnp.einsum("sb,bro->sro", choose_col, every_block, precision=HIGH_PRECISION)
    ).astype(jnp.bfloat16)
    return (input_grad, down_grad, up_grad)


LINE_ORDER = ((3, 2, 1, 0), (3, 2, 0, 1), (0, 1, 3, 2), (0, 1, 2, 3))
PIECES = 2


def grid_shards(
    activations,
    output_gradient,
    frozen_weight,
    adapter_down_maps,
    adapter_up_maps,
    adapter_of_block,
    adapter_grad_slot,
):
    n_row = lax.axis_size("row")
    n_col = lax.axis_size("col")
    row = lax.axis_index("row")
    col = lax.axis_index("col")
    z, y = row // 2, row % 2
    adapters, rank, slab = adapter_down_maps.shape
    width_out = output_gradient.shape[1]
    features = activations.shape[1]
    own_tokens = activations.shape[0]
    own_blocks = own_tokens // BLOCK
    half_tokens = output_gradient.shape[0]
    half_blocks = half_tokens // BLOCK
    blocks = half_blocks * n_col
    order = jnp.array(LINE_ORDER, jnp.int32)[z]
    other_core = [(i, (i + 1) % n_col) for i in range(n_col)]
    other_y = [(i, i ^ 1) for i in range(n_row)]

    chunk = half_tokens // 2
    first = jnp.where(z < 2, 1, 0)
    mine_first = col == first
    own_pairs, got_pairs = [], []
    for i in range(2):
        place = jnp.where(mine_first, order[i], order[2 + i]) - 2 * col
        own = lax.dynamic_slice_in_dim(output_gradient, place * chunk, chunk, 0)
        own_pairs.append(own)
        got_pairs.append(lax.ppermute(own, "col", other_core))
    rows_of = [jnp.where(mine_first, own_pairs[i], got_pairs[i]) for i in range(2)]
    rows_of += [jnp.where(mine_first, got_pairs[i], own_pairs[i]) for i in range(2)]

    def product(p, which_y, piece):
        part = lax.dynamic_slice_in_dim(rows_of[p], which_y * own_tokens, own_tokens, 0)
        width = features // PIECES
        weight = frozen_weight[piece * width : (piece + 1) * width]
        return lax.dot_general(
            part, weight, (((1,), (1,)), ((), ())), preferred_element_type=jnp.float32
        ).astype(jnp.bfloat16)

    def wide(v):
        return v.astype(jnp.float32)

    arrived = {}
    kept = {}
    for p in range(4):
        for piece in range(PIECES):
            arrived[p, piece] = lax.ppermute(product(p, 1 - y, piece), "row", other_y)
        for piece in range(PIECES):
            kept[p, piece] = product(p, y, piece)

    right = {k: [(r, r + 2) for r in range(2 * k)] for k in (1, 2, 3)}
    left = {k: [(n_row - 1 - s, n_row - 1 - d) for s, d in right[k]] for k in (1, 2, 3)}
    totals = []
    for piece in range(PIECES):
        s = [wide(kept[p, piece]) + wide(arrived[p, piece]) for p in range(4)]
        r1 = lax.ppermute(s[0].astype(jnp.bfloat16), "row", right[1])
        l1 = lax.ppermute(s[0].astype(jnp.bfloat16), "row", left[1])
        r2 = jnp.where(z == 0, s[1], s[0]) + wide(r1)
        l2 = jnp.where(z == 3, s[1], s[0]) + wide(l1)
        r2 = lax.ppermute(r2.astype(jnp.bfloat16), "row", right[2])
        l2 = lax.ppermute(l2.astype(jnp.bfloat16), "row", left[2])
        r3 = jnp.where(z == 1, s[1], s[2]) + wide(r2)
        l3 = jnp.where(z == 2, s[1], s[2]) + wide(l2)
        r3 = lax.ppermute(r3.astype(jnp.bfloat16), "row", right[3])
        l3 = lax.ppermute(l3.astype(jnp.bfloat16), "row", left[3])
        totals.append((s[3], r3, l3))

    x_blocks = activations.reshape(own_blocks, BLOCK, features)
    own_dy = output_gradient.reshape(half_blocks, BLOCK, width_out)
    half_adapters = lax.dynamic_slice_in_dim(adapter_of_block, col * half_blocks, half_blocks, 0)
    down_rows = lax.all_to_all(
        adapter_down_maps[adapter_of_block], "row", split_axis=0, concat_axis=2, tiled=True
    )
    back_half = jnp.einsum(
        "bro,bto->brt", adapter_up_maps[half_adapters], own_dy, preferred_element_type=jnp.float32
    )
    back_every = lax.dynamic_update_slice_in_dim(
        jnp.zeros((blocks, rank, BLOCK), jnp.float32), back_half, col * half_blocks, 0
    )
    back_parts = lax.all_to_all(
        back_every.reshape(n_row, own_blocks * rank, BLOCK), "row", split_axis=0, concat_axis=0
    )
    back_own = back_parts.sum(0).reshape(own_blocks, rank, BLOCK)
    hidden_own = jnp.einsum(
        "brd,btd->brt", down_rows, x_blocks, preferred_element_type=jnp.float32
    )
    both = jnp.concatenate([hidden_own, back_own])
    both = both + lax.ppermute(both, "col", other_core)
    hidden_low = both[:own_blocks].astype(jnp.bfloat16)
    back_low = (SCALE * both[own_blocks:]).astype(jnp.bfloat16)
    hidden_all = lax.all_gather(hidden_low, "row", axis=0, tiled=True)

    lora = jnp.einsum("brt,brd->btd", back_low, down_rows, preferred_element_type=jnp.float32)
    lora = lora.reshape(own_tokens, features)
    width = features // PIECES
    input_grad = jnp.concatenate(
        [
            (
                s + wide(r) + wide(l) + lora[:, i * width : (i + 1) * width]
            ).astype(jnp.bfloat16)
            for i, (s, r, l) in enumerate(totals)
        ],
        axis=1,
    )

    slot_of_block = adapter_grad_slot[adapter_of_block]
    down_parts = jnp.einsum(
        "brt,btd->brd", back_low, x_blocks, preferred_element_type=jnp.float32
    ).astype(jnp.bfloat16)
    down_all = lax.all_gather(down_parts, "row", axis=0, tiled=True)
    per_row = adapters // n_row
    own_slots = row * per_row + jnp.arange(per_row, dtype=jnp.int32)
    choose_own = (slot_of_block[None, :] == own_slots[:, None]).astype(jnp.bfloat16)
    down_grad = jnp.einsum("sb,brd->srd", choose_own, down_all, preferred_element_type=jnp.float32)
    down_grad = (down_grad / BLOCK).astype(jnp.bfloat16)

    hidden_half = lax.dynamic_slice_in_dim(hidden_all, col * half_blocks, half_blocks, 0)
    up_parts = jnp.einsum(
        "brt,bto->bro", hidden_half, own_dy, preferred_element_type=jnp.float32
    ).astype(jnp.bfloat16)
    up_got = lax.ppermute(up_parts, "col", other_core)
    per_col = adapters // n_col
    col_slots = col * per_col + jnp.arange(per_col, dtype=jnp.int32)
    choose_col = (slot_of_block[None, :] == col_slots[:, None]).astype(jnp.bfloat16)
    half_slots = jnp.concatenate(
        [
            lax.dynamic_slice_in_dim(choose_col, col * half_blocks, half_blocks, 1),
            lax.dynamic_slice_in_dim(choose_col, (1 - col) * half_blocks, half_blocks, 1),
        ],
        axis=1,
    )
    up_grad = jnp.einsum(
        "sb,bro->sro",
        half_slots,
        jnp.concatenate([up_parts, up_got]),
        preferred_element_type=jnp.float32,
    )
    up_grad = (SCALE / BLOCK * up_grad).astype(jnp.bfloat16)
    return (input_grad, down_grad, up_grad)


def solution(mesh):
    in_specs = (
        P(("groups", "row"), "col"),
        P(("groups", "col"), "row"),
        P("col", "row"),
        P(None, None, ("col", "row")),
        P(None, None, "row"),
        P("groups"),
        P(),
    )
    out_specs = (
        P(("groups", "row"), "col"),
        P(("groups", "row"), None, "col"),
        P(("groups", "col"), None, "row"),
    )
    grid = mesh.shape["row"] == 8 and mesh.shape["col"] == 2
    shards = grid_shards if grid else general_shards
    return jax.shard_map(shards, mesh=mesh, in_specs=in_specs, out_specs=out_specs, check_vma=False)
```

```python
import jax
import jax.numpy as jnp
from jax import lax
from jax.sharding import PartitionSpec as P

BLOCK = 128


SCALE = 2.0
HIGH_PRECISION = lax.Precision.HIGHEST


def general_shards(
    activations,
    output_gradient,
    frozen_weight,
    adapter_down_maps,
    adapter_up_maps,
    adapter_of_block,
    adapter_grad_slot,
):
    n_row = lax.axis_size("row")
    n_col = lax.axis_size("col")
    index_of_row = lax.axis_index("row")
    col_index = lax.axis_index("col")
    adapter_list = adapter_down_maps.shape[0]
    rank_width = adapter_down_maps.shape[1]
    token_slab = adapter_down_maps.shape[2]
    width_out = output_gradient.shape[1]
    half_blocks = output_gradient.shape[0] // BLOCK
    blocks = half_blocks * n_col
    every_token = blocks * BLOCK
    dy_panel = lax.all_gather(output_gradient, "col", axis=0, tiled=True)
    x_columns = lax.all_to_all(activations, "row", split_axis=1, concat_axis=0, tiled=True)
    x_blocks = x_columns.reshape(blocks, BLOCK, token_slab)
    selected_down = adapter_down_maps[adapter_of_block]
    selected_up = adapter_up_maps[adapter_of_block]
    hidden_part = jnp.einsum(
        "btd,brd->btr", x_blocks, selected_down, preferred_element_type=jnp.float32
    )
    own_dy = output_gradient.reshape(half_blocks, BLOCK, width_out)
    own_up = lax.dynamic_slice_in_dim(selected_up, col_index * half_blocks, half_blocks, 0)
    back_own = jnp.einsum("bto,bro->btr", own_dy, own_up, preferred_element_type=jnp.float32)
    back_zero = jnp.zeros((blocks, BLOCK, rank_width), jnp.float32)
    back_part = lax.dynamic_update_slice_in_dim(back_zero, back_own, col_index * half_blocks, 0)
    hidden, back_sum = lax.psum((hidden_part, back_part), ("row", "col"))
    back = SCALE * back_sum
    hidden_low = hidden.astype(jnp.bfloat16)
    backward_low_rank = back.astype(jnp.bfloat16)
    adapter_token_slab = jnp.einsum(
        "efs,esl->efl", backward_low_rank, selected_down, preferred_element_type=jnp.float32
    )
    adapter_token_slab = adapter_token_slab.reshape(every_token, token_slab)
    partial_term = lax.dot_general(
        dy_panel, frozen_weight, (((1,), (1,)), ((), ())), preferred_element_type=jnp.float32
    )
    present_value = lax.dynamic_slice_in_dim(partial_term, index_of_row * token_slab, token_slab, 1)
    input_grad = lax.psum_scatter(
        lax.dynamic_update_slice_in_dim(
            partial_term, present_value + adapter_token_slab, index_of_row * token_slab, 1
        ).astype(jnp.bfloat16),
        "row",
        scatter_dimension=0,
        tiled=True,
    )
    slot_of_block = adapter_grad_slot[adapter_of_block]
    down_parts = jnp.einsum(
        "btr,btd->brd", backward_low_rank, x_blocks, preferred_element_type=jnp.float32
    )
    per_row = adapter_list // n_row
    own_slots = index_of_row * per_row + jnp.arange(per_row, dtype=jnp.int32)
    choose_own = (slot_of_block[None, :] == own_slots[:, None]).astype(jnp.float32)
    summed = jnp.einsum(
        "sb,brd->srd",
        choose_own,
        lax.all_gather(down_parts.astype(jnp.bfloat16), "row", axis=2, tiled=True).astype(
            jnp.float32
        ),
        precision=HIGH_PRECISION,
    )
    down_grad = (summed / BLOCK).astype(jnp.bfloat16)
    own_hidden = lax.dynamic_slice_in_dim(hidden_low, col_index * half_blocks, half_blocks, 0)
    own_cotangent = output_gradient.reshape(half_blocks, BLOCK, width_out)
    up_parts = jnp.einsum(
        "btr,bto->bro", own_hidden, own_cotangent, preferred_element_type=jnp.float32
    )
    every_block = lax.all_gather(up_parts.astype(jnp.bfloat16), "col", axis=0, tiled=True).astype(
        up_parts.dtype
    )
    per_col = adapter_list // n_col
    col_slots = col_index * per_col + jnp.arange(per_col, dtype=jnp.int32)
    choose_col = (slot_of_block[None, :] == col_slots[:, None]).astype(jnp.float32)
    up_grad = (
        SCALE / BLOCK * jnp.einsum("sb,bro->sro", choose_col, every_block, precision=HIGH_PRECISION)
    ).astype(jnp.bfloat16)
    return (input_grad, down_grad, up_grad)


LINE_ORDER = ((3, 2, 1, 0), (3, 2, 0, 1), (0, 1, 3, 2), (0, 1, 2, 3))
PIECES = 2
AHEAD = 3


def grid_shards(
    activations,
    output_gradient,
    frozen_weight,
    adapter_down_maps,
    adapter_up_maps,
    adapter_of_block,
    adapter_grad_slot,
):
    n_row = lax.axis_size("row")
    n_col = lax.axis_size("col")
    row = lax.axis_index("row")
    col = lax.axis_index("col")
    z, y = row // 2, row % 2
    adapters, rank, slab = adapter_down_maps.shape
    width_out = output_gradient.shape[1]
    features = activations.shape[1]
    own_tokens = activations.shape[0]
    own_blocks = own_tokens // BLOCK
    half_tokens = output_gradient.shape[0]
    half_blocks = half_tokens // BLOCK
    blocks = half_blocks * n_col
    order = jnp.array(LINE_ORDER, jnp.int32)[z]
    other_core = [(i, (i + 1) % n_col) for i in range(n_col)]
    other_y = [(i, i ^ 1) for i in range(n_row)]

    chunk = half_tokens // 2
    first = jnp.where(z < 2, 1, 0)
    mine_first = col == first
    own_pairs, got_pairs = [], []
    for i in range(2):
        place = jnp.where(mine_first, order[i], order[2 + i]) - 2 * col
        own = lax.dynamic_slice_in_dim(output_gradient, place * chunk, chunk, 0)
        own_pairs.append(own)
        got_pairs.append(lax.ppermute(own, "col", other_core))
    rows_of = [jnp.where(mine_first, own_pairs[i], got_pairs[i]) for i in range(2)]
    rows_of += [jnp.where(mine_first, got_pairs[i], own_pairs[i]) for i in range(2)]

    def wide(v):
        return v.astype(jnp.float32)

    def narrow(v):
        return v.astype(jnp.bfloat16)

    def after(value, *others):
        return lax.optimization_barrier((value,) + others)[0]

    def times(rows, start, width):
        return narrow(
            lax.dot_general(
                rows,
                frozen_weight[start : start + width],
                (((1,), (1,)), ((), ())),
                preferred_element_type=jnp.float32,
            )
        )

    right = {k: [(r, r + 2) for r in range(2 * k)] for k in (1, 2, 3)}
    left = {k: [(n_row - 1 - s, n_row - 1 - d) for s, d in right[k]] for k in (1, 2, 3)}

    def line_step(k, s, r, l):
        if k == 1:
            to_right, to_left = s[0], s[0]
        elif k == 2:
            to_right = jnp.where(z == 0, s[1], s[0]) + wide(r)
            to_left = jnp.where(z == 3, s[1], s[0]) + wide(l)
        else:
            to_right = jnp.where(z == 1, s[1], s[2]) + wide(r)
            to_left = jnp.where(z == 2, s[1], s[2]) + wide(l)
        return (
            lax.ppermute(narrow(to_right), "row", right[k]),
            lax.ppermute(narrow(to_left), "row", left[k]),
        )

    def rows_for(p, which_y):
        return lax.dynamic_slice_in_dim(rows_of[p], which_y * own_tokens, own_tokens, 0)

    turned = features // 8
    width = (features - turned) // PIECES
    starts = [i * width for i in range(PIECES)]
    last = features - turned
    arrived, kept, line, sums = {}, {}, {}, {}
    flights = []
    turned_parts, turned_line = [], (None, None)
    for p in range(4):
        away, here = rows_for(p, 1 - y), rows_for(p, y)
        for i in range(PIECES):
            rows = after(away, *flights[-AHEAD:][:1]) if len(flights) >= AHEAD else away
            arrived[p, i] = lax.ppermute(times(rows, starts[i], width), "row", other_y)
            flights.append(arrived[p, i])
        gate = flights[-3:-2]
        behind = flights[-4:-3] or flights[:1]
        turned_parts.append(wide(times(after(rows_of[p], *gate), last, turned)))
        if p < 3:
            turned_line = line_step(p + 1, turned_parts, *turned_line)
        for i in range(PIECES):
            kept[p, i] = times(after(here, *behind), starts[i], width)
            sums[p, i] = wide(kept[p, i]) + wide(arrived[p, i])
            if p < 3:
                s = [sums[q, i] for q in range(p + 1)]
                line[i] = line_step(p + 1, s, *line.get(i, (None, None)))
    turned_sum = turned_parts[3] + wide(turned_line[0]) + wide(turned_line[1])
    turned_away = lax.dynamic_slice_in_dim(turned_sum, (1 - y) * own_tokens, own_tokens, 0)
    turned_here = lax.dynamic_slice_in_dim(turned_sum, y * own_tokens, own_tokens, 0)
    turned_sum = turned_here + wide(lax.ppermute(narrow(turned_away), "row", other_y))
    grads = [sums[3, i] + wide(line[i][0]) + wide(line[i][1]) for i in range(PIECES)]
    grads.append(turned_sum)

    output_late, adapter_of_late, activations_late = lax.optimization_barrier(
        (output_gradient, adapter_of_block, activations, flights[0])
    )[:3]

    x_blocks = activations_late.reshape(own_blocks, BLOCK, features)
    own_dy = output_late.reshape(half_blocks, BLOCK, width_out)
    half_adapters = lax.dynamic_slice_in_dim(adapter_of_late, col * half_blocks, half_blocks, 0)
    down_rows = lax.all_to_all(
        adapter_down_maps[adapter_of_late], "row", split_axis=0, concat_axis=2, tiled=True
    )
    back_half = jnp.einsum(
        "bro,bto->brt", adapter_up_maps[half_adapters], own_dy, preferred_element_type=jnp.float32
    )
    back_every = lax.dynamic_update_slice_in_dim(
        jnp.zeros((blocks, rank, BLOCK), jnp.float32), back_half, col * half_blocks, 0
    )
    back_parts = lax.all_to_all(
        back_every.reshape(n_row, own_blocks * rank, BLOCK), "row", split_axis=0, concat_axis=0
    )
    back_own = back_parts.sum(0).reshape(own_blocks, rank, BLOCK)
    hidden_own = jnp.einsum(
        "brd,btd->brt", down_rows, x_blocks, preferred_element_type=jnp.float32
    )
    both = jnp.concatenate([hidden_own, back_own])
    both = both + lax.ppermute(both, "col", other_core)
    hidden_low = both[:own_blocks].astype(jnp.bfloat16)
    back_low = (SCALE * both[own_blocks:]).astype(jnp.bfloat16)
    hidden_all = lax.all_gather(hidden_low, "row", axis=0, tiled=True)

    lora = jnp.einsum("brt,brd->btd", back_low, down_rows, preferred_element_type=jnp.float32)
    lora = lora.reshape(own_tokens, features)
    ends = starts[1:] + [last, features]
    input_grad = jnp.concatenate(
        [
            narrow(g + lora[:, begin:end])
            for g, begin, end in zip(grads, starts + [last], ends)
        ],
        axis=1,
    )

    slot_of_block = adapter_grad_slot[adapter_of_late]
    down_parts = jnp.einsum(
        "brt,btd->brd", back_low, x_blocks, preferred_element_type=jnp.float32
    ).astype(jnp.bfloat16)
    down_all = lax.all_gather(down_parts, "row", axis=0, tiled=True)
    per_row = adapters // n_row
    own_slots = row * per_row + jnp.arange(per_row, dtype=jnp.int32)
    choose_own = (slot_of_block[None, :] == own_slots[:, None]).astype(jnp.bfloat16)
    down_grad = jnp.einsum("sb,brd->srd", choose_own, down_all, preferred_element_type=jnp.float32)
    down_grad = (down_grad / BLOCK).astype(jnp.bfloat16)

    hidden_half = lax.dynamic_slice_in_dim(hidden_all, col * half_blocks, half_blocks, 0)
    up_parts = jnp.einsum(
        "brt,bto->bro", hidden_half, own_dy, preferred_element_type=jnp.float32
    ).astype(jnp.bfloat16)
    up_got = lax.ppermute(up_parts, "col", other_core)
    per_col = adapters // n_col
    col_slots = col * per_col + jnp.arange(per_col, dtype=jnp.int32)
    choose_col = (slot_of_block[None, :] == col_slots[:, None]).astype(jnp.bfloat16)
    half_slots = jnp.concatenate(
        [
            lax.dynamic_slice_in_dim(choose_col, col * half_blocks, half_blocks, 1),
            lax.dynamic_slice_in_dim(choose_col, (1 - col) * half_blocks, half_blocks, 1),
        ],
        axis=1,
    )
    up_grad = jnp.einsum(
        "sb,bro->sro",
        half_slots,
        jnp.concatenate([up_parts, up_got]),
        preferred_element_type=jnp.float32,
    )
    up_grad = (SCALE / BLOCK * up_grad).astype(jnp.bfloat16)
    return (input_grad, down_grad, up_grad)


def solution(mesh):
    in_specs = (
        P(("groups", "row"), "col"),
        P(("groups", "col"), "row"),
        P("col", "row"),
        P(None, None, ("col", "row")),
        P(None, None, "row"),
        P("groups"),
        P(),
    )
    out_specs = (
        P(("groups", "row"), "col"),
        P(("groups", "row"), None, "col"),
        P(("groups", "col"), None, "row"),
    )
    grid = mesh.shape["row"] == 8 and mesh.shape["col"] == 2
    shards = grid_shards if grid else general_shards
    return jax.shard_map(shards, mesh=mesh, in_specs=in_specs, out_specs=out_specs, check_vma=False)
```

```python
import jax
import jax.numpy as jnp
from jax import lax
from jax.sharding import PartitionSpec as P

BLOCK = 128


SCALE = 2.0
HIGH_PRECISION = lax.Precision.HIGHEST


def general_shards(
    activations,
    output_gradient,
    frozen_weight,
    adapter_down_maps,
    adapter_up_maps,
    adapter_of_block,
    adapter_grad_slot,
):
    n_row = lax.axis_size("row")
    n_col = lax.axis_size("col")
    index_of_row = lax.axis_index("row")
    col_index = lax.axis_index("col")
    adapter_list = adapter_down_maps.shape[0]
    rank_width = adapter_down_maps.shape[1]
    token_slab = adapter_down_maps.shape[2]
    width_out = output_gradient.shape[1]
    half_blocks = output_gradient.shape[0] // BLOCK
    blocks = half_blocks * n_col
    every_token = blocks * BLOCK
    dy_panel = lax.all_gather(output_gradient, "col", axis=0, tiled=True)
    x_columns = lax.all_to_all(activations, "row", split_axis=1, concat_axis=0, tiled=True)
    x_blocks = x_columns.reshape(blocks, BLOCK, token_slab)
    selected_down = adapter_down_maps[adapter_of_block]
    selected_up = adapter_up_maps[adapter_of_block]
    hidden_part = jnp.einsum(
        "btd,brd->btr", x_blocks, selected_down, preferred_element_type=jnp.float32
    )
    own_dy = output_gradient.reshape(half_blocks, BLOCK, width_out)
    own_up = lax.dynamic_slice_in_dim(selected_up, col_index * half_blocks, half_blocks, 0)
    back_own = jnp.einsum("bto,bro->btr", own_dy, own_up, preferred_element_type=jnp.float32)
    back_zero = jnp.zeros((blocks, BLOCK, rank_width), jnp.float32)
    back_part = lax.dynamic_update_slice_in_dim(back_zero, back_own, col_index * half_blocks, 0)
    hidden, back_sum = lax.psum((hidden_part, back_part), ("row", "col"))
    back = SCALE * back_sum
    hidden_low = hidden.astype(jnp.bfloat16)
    backward_low_rank = back.astype(jnp.bfloat16)
    adapter_token_slab = jnp.einsum(
        "efs,esl->efl", backward_low_rank, selected_down, preferred_element_type=jnp.float32
    )
    adapter_token_slab = adapter_token_slab.reshape(every_token, token_slab)
    partial_term = lax.dot_general(
        dy_panel, frozen_weight, (((1,), (1,)), ((), ())), preferred_element_type=jnp.float32
    )
    present_value = lax.dynamic_slice_in_dim(partial_term, index_of_row * token_slab, token_slab, 1)
    input_grad = lax.psum_scatter(
        lax.dynamic_update_slice_in_dim(
            partial_term, present_value + adapter_token_slab, index_of_row * token_slab, 1
        ).astype(jnp.bfloat16),
        "row",
        scatter_dimension=0,
        tiled=True,
    )
    slot_of_block = adapter_grad_slot[adapter_of_block]
    down_parts = jnp.einsum(
        "btr,btd->brd", backward_low_rank, x_blocks, preferred_element_type=jnp.float32
    )
    per_row = adapter_list // n_row
    own_slots = index_of_row * per_row + jnp.arange(per_row, dtype=jnp.int32)
    choose_own = (slot_of_block[None, :] == own_slots[:, None]).astype(jnp.float32)
    summed = jnp.einsum(
        "sb,brd->srd",
        choose_own,
        lax.all_gather(down_parts.astype(jnp.bfloat16), "row", axis=2, tiled=True).astype(
            jnp.float32
        ),
        precision=HIGH_PRECISION,
    )
    down_grad = (summed / BLOCK).astype(jnp.bfloat16)
    own_hidden = lax.dynamic_slice_in_dim(hidden_low, col_index * half_blocks, half_blocks, 0)
    own_cotangent = output_gradient.reshape(half_blocks, BLOCK, width_out)
    up_parts = jnp.einsum(
        "btr,bto->bro", own_hidden, own_cotangent, preferred_element_type=jnp.float32
    )
    every_block = lax.all_gather(up_parts.astype(jnp.bfloat16), "col", axis=0, tiled=True).astype(
        up_parts.dtype
    )
    per_col = adapter_list // n_col
    col_slots = col_index * per_col + jnp.arange(per_col, dtype=jnp.int32)
    choose_col = (slot_of_block[None, :] == col_slots[:, None]).astype(jnp.float32)
    up_grad = (
        SCALE / BLOCK * jnp.einsum("sb,bro->sro", choose_col, every_block, precision=HIGH_PRECISION)
    ).astype(jnp.bfloat16)
    return (input_grad, down_grad, up_grad)


LINE_ORDER = ((3, 2, 1, 0), (3, 2, 0, 1), (0, 1, 3, 2), (0, 1, 2, 3))
PIECES = 1
AHEAD = 2


def grid_shards(
    activations,
    output_gradient,
    frozen_weight,
    adapter_down_maps,
    adapter_up_maps,
    adapter_of_block,
    adapter_grad_slot,
):
    n_row = lax.axis_size("row")
    n_col = lax.axis_size("col")
    row = lax.axis_index("row")
    col = lax.axis_index("col")
    z, y = row // 2, row % 2
    adapters, rank, slab = adapter_down_maps.shape
    width_out = output_gradient.shape[1]
    features = activations.shape[1]
    own_tokens = activations.shape[0]
    own_blocks = own_tokens // BLOCK
    half_tokens = output_gradient.shape[0]
    half_blocks = half_tokens // BLOCK
    blocks = half_blocks * n_col
    order = jnp.array(LINE_ORDER, jnp.int32)[z]
    other_core = [(i, (i + 1) % n_col) for i in range(n_col)]
    other_y = [(i, i ^ 1) for i in range(n_row)]

    chunk = half_tokens // 2
    first = jnp.where(z < 2, 1, 0)
    mine_first = col == first
    own_pairs, got_pairs = [], []
    for i in range(2):
        place = jnp.where(mine_first, order[i], order[2 + i]) - 2 * col
        own = lax.dynamic_slice_in_dim(output_gradient, place * chunk, chunk, 0)
        own_pairs.append(own)
        got_pairs.append(lax.ppermute(own, "col", other_core))
    rows_of = [jnp.where(mine_first, own_pairs[i], got_pairs[i]) for i in range(2)]
    rows_of += [jnp.where(mine_first, got_pairs[i], own_pairs[i]) for i in range(2)]

    def wide(v):
        return v.astype(jnp.float32)

    def narrow(v):
        return v.astype(jnp.bfloat16)

    def after(value, *others):
        return lax.optimization_barrier((value,) + others)[0]

    def times(rows, start, width):
        return narrow(
            lax.dot_general(
                rows,
                frozen_weight[start : start + width],
                (((1,), (1,)), ((), ())),
                preferred_element_type=jnp.float32,
            )
        )

    right = {k: [(r, r + 2) for r in range(2 * k)] for k in (1, 2, 3)}
    left = {k: [(n_row - 1 - s, n_row - 1 - d) for s, d in right[k]] for k in (1, 2, 3)}

    def line_step(k, s, r, l):
        if k == 1:
            to_right, to_left = s[0], s[0]
        elif k == 2:
            to_right = jnp.where(z == 0, s[1], s[0]) + wide(r)
            to_left = jnp.where(z == 3, s[1], s[0]) + wide(l)
        else:
            to_right = jnp.where(z == 1, s[1], s[2]) + wide(r)
            to_left = jnp.where(z == 2, s[1], s[2]) + wide(l)
        return (
            lax.ppermute(narrow(to_right), "row", right[k]),
            lax.ppermute(narrow(to_left), "row", left[k]),
        )

    def rows_for(p, which_y):
        return lax.dynamic_slice_in_dim(rows_of[p], which_y * own_tokens, own_tokens, 0)

    width = features // PIECES
    starts = [i * width for i in range(PIECES)]
    arrived, kept, line, sums = {}, {}, {}, {}
    flights = []
    for p in range(4):
        away, here = rows_for(p, 1 - y), rows_for(p, y)
        for i in range(PIECES):
            rows = after(away, *flights[-AHEAD:][:1]) if len(flights) >= AHEAD else away
            sent = times(rows, starts[i], width)
            arrived[p, i] = lax.ppermute(sent, "row", other_y)
            flights.append(arrived[p, i])
        behind = flights[PIECES * (p - 1) :][:1] if p > 1 else [sent]
        for i in range(PIECES):
            kept[p, i] = times(after(here, *behind), starts[i], width)
            sums[p, i] = wide(kept[p, i]) + wide(arrived[p, i])
            if p < 3:
                s = [sums[q, i] for q in range(p + 1)]
                line[i] = line_step(p + 1, s, *line.get(i, (None, None)))
    grads = [sums[3, i] + wide(line[i][0]) + wide(line[i][1]) for i in range(PIECES)]

    output_late, adapter_of_late, activations_late = lax.optimization_barrier(
        (output_gradient, adapter_of_block, activations, flights[0])
    )[:3]

    x_blocks = activations_late.reshape(own_blocks, BLOCK, features)
    own_dy = output_late.reshape(half_blocks, BLOCK, width_out)
    half_adapters = lax.dynamic_slice_in_dim(adapter_of_late, col * half_blocks, half_blocks, 0)
    down_rows = lax.all_to_all(
        adapter_down_maps[adapter_of_late], "row", split_axis=0, concat_axis=2, tiled=True
    )
    back_half = jnp.einsum(
        "bro,bto->brt", adapter_up_maps[half_adapters], own_dy, preferred_element_type=jnp.float32
    )
    back_every = lax.dynamic_update_slice_in_dim(
        jnp.zeros((blocks, rank, BLOCK), jnp.float32), back_half, col * half_blocks, 0
    )
    back_parts = lax.all_to_all(
        back_every.reshape(n_row, own_blocks * rank, BLOCK), "row", split_axis=0, concat_axis=0
    )
    back_own = back_parts.sum(0).reshape(own_blocks, rank, BLOCK)
    hidden_own = jnp.einsum(
        "brd,btd->brt", down_rows, x_blocks, preferred_element_type=jnp.float32
    )
    both = jnp.concatenate([hidden_own, back_own])
    both = both + lax.ppermute(both, "col", other_core)
    hidden_low = both[:own_blocks].astype(jnp.bfloat16)
    back_low = (SCALE * both[own_blocks:]).astype(jnp.bfloat16)
    hidden_all = lax.all_to_all(
        jnp.broadcast_to(hidden_low, (n_row,) + hidden_low.shape), "row", split_axis=0, concat_axis=0
    ).reshape(blocks, rank, BLOCK)

    lora = jnp.einsum("brt,brd->btd", back_low, down_rows, preferred_element_type=jnp.float32)
    lora = lora.reshape(own_tokens, features)
    ends = starts[1:] + [features]
    input_grad = jnp.concatenate(
        [
            narrow(g + lora[:, begin:end])
            for g, begin, end in zip(grads, starts, ends)
        ],
        axis=1,
    )

    slot_of_block = adapter_grad_slot[adapter_of_late]
    down_parts = jnp.einsum(
        "brt,btd->brd", back_low, x_blocks, preferred_element_type=jnp.float32
    ).astype(jnp.bfloat16)
    down_all = lax.all_gather(down_parts, "row", axis=0, tiled=True)
    per_row = adapters // n_row
    own_slots = row * per_row + jnp.arange(per_row, dtype=jnp.int32)
    choose_own = (slot_of_block[None, :] == own_slots[:, None]).astype(jnp.bfloat16)
    down_grad = jnp.einsum("sb,brd->srd", choose_own, down_all, preferred_element_type=jnp.float32)
    down_grad = (down_grad / BLOCK).astype(jnp.bfloat16)

    hidden_half = lax.dynamic_slice_in_dim(hidden_all, col * half_blocks, half_blocks, 0)
    up_parts = jnp.einsum(
        "brt,bto->bro", hidden_half, own_dy, preferred_element_type=jnp.float32
    ).astype(jnp.bfloat16)
    up_got = lax.ppermute(up_parts, "col", other_core)
    per_col = adapters // n_col
    col_slots = col * per_col + jnp.arange(per_col, dtype=jnp.int32)
    choose_col = (slot_of_block[None, :] == col_slots[:, None]).astype(jnp.bfloat16)
    half_slots = jnp.concatenate(
        [
            lax.dynamic_slice_in_dim(choose_col, col * half_blocks, half_blocks, 1),
            lax.dynamic_slice_in_dim(choose_col, (1 - col) * half_blocks, half_blocks, 1),
        ],
        axis=1,
    )
    up_grad = jnp.einsum(
        "sb,bro->sro",
        half_slots,
        jnp.concatenate([up_parts, up_got]),
        preferred_element_type=jnp.float32,
    )
    up_grad = (SCALE / BLOCK * up_grad).astype(jnp.bfloat16)
    return (input_grad, down_grad, up_grad)


def solution(mesh):
    in_specs = (
        P(("groups", "row"), "col"),
        P(("groups", "col"), "row"),
        P("col", "row"),
        P(None, None, ("col", "row")),
        P(None, None, "row"),
        P("groups"),
        P(),
    )
    out_specs = (
        P(("groups", "row"), "col"),
        P(("groups", "row"), None, "col"),
        P(("groups", "col"), None, "row"),
    )
    grid = mesh.shape["row"] == 8 and mesh.shape["col"] == 2
    shards = grid_shards if grid else general_shards
    return jax.shard_map(shards, mesh=mesh, in_specs=in_specs, out_specs=out_specs, check_vma=False)
```
